512 devices in a mesh: rep: 4 (over x), expert: 128 (over z, y, core).
Axes of the slice: x: 4, y: 8, z: 8, core: 2. Of those that a mesh axis runs over, the one named last changes fastest.
Arguments:
- tokens: bfloat16 [65536, 1536], P(('rep', 'expert')), may hold values from -6 to 6
- routes: int32 [65536, 4], P(('rep', 'expert')), may hold values from 0 to 127, all different within a row; in each aligned block of 128 rows (0 to 127, 128 to 255, ...) at most 5 rows name the same one
- gates: bfloat16 [65536, 4], P(('rep', 'expert')), may hold values from 0.049804688 to 1
- output_grad: bfloat16 [65536, 1536], P(('rep', 'expert')), may hold values from -6 to 6
- w_in: bfloat16 [128, 1536, 768], P('expert', 'rep'), may hold values from -0.15625 to 0.15625
- w_out: bfloat16 [128, 384, 1536], P('expert', None, 'rep'), may hold values from -0.3125 to 0.3125
- momentum_in: bfloat16 [128, 1536, 768], P('expert', 'rep'), may hold values from -24 to 24
- momentum_out: bfloat16 [128, 384, 1536], P('expert', None, 'rep'), may hold values from -24 to 24
Outputs:
- token_grad: bfloat16 [65536, 1536], P(('rep', 'expert'))
- gate_grad: bfloat16 [65536, 4], P(('rep', 'expert'))
- new_momentum_in: bfloat16 [128, 1536, 768], P('expert', 'rep')
- new_momentum_out: bfloat16 [128, 384, 1536], P('expert', None, 'rep')
The draws below stay inside these ranges and needn't reach their ends.
Inputs may be any that keep to these rules, and one draw needn't show every extreme that they name: `routes`: each row names 4 different experts. Within the 128 rows of one device no expert is named by more than 5 rows, and on some devices one expert is named by exactly 5 rows.
All inputs are finite; a program needn't handle non-finite values.
Results may differ from the reference program's by a relative error of at most 0.012.
Values may be sent and summed in bfloat16 or wider, within the bound.
A program may use at most 64 MiB of HBM per device.

```python
import math
import jax
import jax.numpy as jnp
import numpy as np
from jax import lax

D = 1536
FFN = 384
TOP = 4
TOK_DEV = 128
EXPERTS = 128
CAP = 5
TOKENS = 65536
N_REP = 4
N_EXPERT = 128


def block_levels(stream_key, extent, cuts, least, high):
    def one(position, parts):
        heights = jax.random.uniform(jax.random.fold_in(jax.random.fold_in(stream_key, 6), position), (parts,), jnp.float32, least / len(cuts), high / len(cuts))
        return jnp.repeat(jnp.exp(heights), extent[position] // parts).reshape((-1,) + (1,) * (len(extent) - position - 1))

    level = one(*cuts[0])
    for cut in cuts[1:]:
        level = level * one(*cut)
    return level


def deal_out(own_key, own, number, rows, count, top, reach, lean):
    order = jax.random.permutation(own_key, count)
    crowded, usual = portions_of(count, rows * top, reach, lean, True), portions_of(count, rows * top, reach, lean, False)
    places = jnp.arange(count)

    def named(lengths, turn):
        used = int((lengths > 0).sum())
        fixed = max(1, used // 4)
        passed = fixed + (places - fixed + turn * (used - fixed)) % max(1, count - fixed)
        return jnp.zeros((count,), jnp.int32).at[order[jnp.where(places < fixed, places, passed)]].set(jnp.asarray(lengths, jnp.int32))

    lengths = jnp.where(number % 4 == 0, named(crowded, number // 4), named(usual, number - number // 4 - 1))
    mixed = jax.random.permutation(jax.random.fold_in(own, 3), count)
    giver, taker = mixed[0:count // 2 * 2:2], mixed[1:count // 2 * 2:2]
    room = jnp.minimum(lengths[giver] - 1, reach - lengths[taker]) // 2
    room = jnp.where((giver == order[0]) | (taker == order[0]) | (lengths[taker] == 0), 0, jnp.maximum(room, 0))
    passed = jax.random.randint(jax.random.fold_in(own, 4), (count // 2,), 0, 1 << 20) % (room + 1)
    lengths = lengths.at[giver].add(-passed).at[taker].add(passed)
    items = jnp.searchsorted(jnp.cumsum(lengths), jnp.arange(rows * top), side="right").astype(jnp.int32)
    listing = items.reshape(top, rows).T
    listing = listing[jax.random.permutation(jax.random.fold_in(own, 1), rows)]
    turn = jax.random.randint(jax.random.fold_in(own, 2), (rows, 1), 0, top)
    return jnp.take_along_axis(listing, (jnp.arange(top)[None, :] + turn) % top, axis=1)


def portions_of(amount, total, reach, slope, full):
    portions = [(1 << 20) // math.isqrt(standing ** slope) + 1 for standing in range(1, amount + 1)]
    largest = reach if full else min(reach, max(-(-total // amount), total * portions[0] // sum(portions)))
    least = 1 if total - largest >= amount - 1 else 0
    counts, rest = [largest] + [least] * (amount - 1), total - largest - least * (amount - 1)
    while rest > 0:
        movable = [i for i in range(1, amount) if counts[i] < largest] or [i for i in range(1, amount) if counts[i] < reach]
        mass, left = sum([portions[i] for i in movable]), rest
        for i in movable:
            more = min(reach - counts[i], max(1, left * portions[i] // mass), rest)
            counts[i] = counts[i] + more
            rest = rest - more
    return np.array(counts)


def centred(key, shape, spread, reach, cuts=(), held_as=jnp.bfloat16):
    entries = jax.random.normal(key, shape, jnp.float32) * spread
    if len(cuts) > 0:
        entries = block_levels(key, shape, cuts, -0.22, 0.18) * entries
    return jnp.clip(entries, min=-reach, max=reach).astype(held_as)


def setup_inputs(seed: int = 0) -> dict:
    key_of = jax.random.split(jax.random.key(seed), 9)
    tokens = centred(key_of[0], (TOKENS, D), 1.0, 6.0, ((0, 512),))
    routes_keys = jax.random.split(jax.random.fold_in(key_of[1], 1), TOKENS // TOK_DEV)
    routes_turns = jax.random.permutation(jax.random.fold_in(key_of[1], 3), TOKENS // TOK_DEV)
    routes = jax.vmap(lambda own, number: deal_out(jax.random.fold_in(key_of[1], 2), own, number, TOK_DEV, EXPERTS, TOP, CAP, 2))(routes_keys, routes_turns).reshape((TOKENS, TOP))
    gates = jnp.clip(jnp.exp(math.log(1.0) - 2.9996462 * jax.random.uniform(key_of[2], (TOKENS, TOP), jnp.float32) ** block_levels(key_of[2], (TOKENS, TOP), ((0, 512),), -0.2, 0.2)), 0.049804688, 1.0).astype(jnp.bfloat16)
    output_grad = centred(key_of[3], (TOKENS, D), 1.0, 6.0, ((0, 512),))
    w_in = centred(key_of[4], (EXPERTS, D, 2 * FFN), D ** -0.5, 0.15625, ((0, 128), (1, 4)))
    w_out = centred(key_of[5], (EXPERTS, FFN, D), FFN ** -0.5, 0.3125, ((0, 128), (2, 4)))
    momentum_in = centred(key_of[6], (EXPERTS, D, 2 * FFN), 4.0, 24.0, ((0, 128), (1, 4)))
    momentum_out = centred(key_of[7], (EXPERTS, FFN, D), 4.0, 24.0, ((0, 128), (2, 4)))
    return {"tokens": tokens, "routes": routes, "gates": gates, "output_grad": output_grad, "w_in": w_in, "w_out": w_out, "momentum_in": momentum_in, "momentum_out": momentum_out}


def slot_positions(routes):
    flat_routes = routes.reshape(-1)
    one_hot = (flat_routes[:, None] == jnp.arange(EXPERTS, dtype=jnp.int32)[None, :]).astype(jnp.int32)
    earlier = jnp.cumsum(one_hot, axis=0) - one_hot
    return jnp.sum(earlier * one_hot, axis=1).reshape(routes.shape).astype(jnp.int32)


def expert_pass(x_rows, grad_rows, gate_rows, weight_in, weight_out):
    width_ffn = weight_out.shape[0]
    both = jnp.dot(x_rows, weight_in, preferred_element_type=jnp.float32)
    gate_pre = both[:, :width_ffn]
    up_part = both[:, width_ffn:]
    silu_gate = jax.nn.silu(gate_pre)
    hidden = (silu_gate * up_part).astype(jnp.bfloat16)
    expert_out = jnp.dot(hidden, weight_out, preferred_element_type=jnp.float32)
    gate_grad = jnp.sum(expert_out * grad_rows.astype(jnp.float32), axis=1).astype(jnp.bfloat16)
    scaled = (gate_rows.astype(jnp.float32)[:, None] * grad_rows.astype(jnp.float32)).astype(jnp.bfloat16)
    hidden_grad = jnp.dot(scaled, weight_out.T, preferred_element_type=jnp.float32)
    sigma = jax.nn.sigmoid(gate_pre)
    dgu = jnp.concatenate([hidden_grad * up_part * sigma * (1.0 + gate_pre * (1.0 - sigma)), hidden_grad * silu_gate], axis=1).astype(jnp.bfloat16)
    row_grad = jnp.dot(dgu, weight_in.T, preferred_element_type=jnp.float32).astype(jnp.bfloat16)
    part_in = jnp.dot(x_rows.T, dgu, preferred_element_type=jnp.float32).astype(jnp.bfloat16)
    part_out = jnp.dot(hidden.T, scaled, preferred_element_type=jnp.float32).astype(jnp.bfloat16)
    return row_grad, gate_grad, part_in, part_out


def reference(tokens, routes, gates, output_grad, w_in, w_out, momentum_in, momentum_out):
    blocks = N_EXPERT
    per_group = blocks * TOK_DEV
    width = tokens.shape[1]
    sums_in = jnp.zeros(w_in.shape, jnp.float32)
    sums_out = jnp.zeros(w_out.shape, jnp.float32)
    grad_parts = []
    gate_parts = []
    for group in range(N_REP):
        first = group * per_group
        x_group = tokens[first:first + per_group]
        route_group = routes[first:first + per_group]
        gate_group = gates[first:first + per_group]
        dy_group = output_grad[first:first + per_group]
        slots = jax.vmap(slot_positions)(route_group.reshape(blocks, TOK_DEV, TOP)).reshape(per_group, TOP)
        owner = jnp.broadcast_to((jnp.arange(per_group, dtype=jnp.int32) // TOK_DEV)[:, None], (per_group, TOP)).astype(jnp.int32)
        token_ids = jnp.broadcast_to(jnp.arange(per_group, dtype=jnp.int32)[:, None], (per_group, TOP)).astype(jnp.int32)
        choice_ids = jnp.broadcast_to(jnp.arange(TOP, dtype=jnp.int32)[None, :], (per_group, TOP)).astype(jnp.int32)
        table = jnp.full((EXPERTS, blocks, CAP), per_group, jnp.int32).at[route_group, owner, slots].set(token_ids)
        choice_table = jnp.zeros((EXPERTS, blocks, CAP), jnp.int32).at[route_group, owner, slots].set(choice_ids)
        gate_table = jnp.zeros((EXPERTS, blocks, CAP), jnp.bfloat16).at[route_group, owner, slots].set(gate_group)
        zero_row = jnp.zeros((1, width), jnp.bfloat16)
        x_padded = jnp.concatenate([x_group, zero_row], axis=0)
        dy_padded = jnp.concatenate([dy_group, zero_row], axis=0)

        def one_expert(inputs):
            expert_table, expert_gates, weight_in, weight_out = inputs
            picked = expert_table.reshape(-1)
            return expert_pass(x_padded[picked], dy_padded[picked], expert_gates.reshape(-1), weight_in, weight_out)

        row_grads, gate_grads, parts_in, parts_out = lax.map(one_expert, (table, gate_table, w_in, w_out))
        sums_in = sums_in + parts_in.astype(jnp.float32)
        sums_out = sums_out + parts_out.astype(jnp.float32)
        flat_tokens = table.reshape(-1)
        flat_choices = choice_table.reshape(-1)
        token_sum = jnp.zeros((per_group + 1, width), jnp.float32).at[flat_tokens].add(row_grads.reshape(-1, width).astype(jnp.float32))
        grad_parts.append(token_sum[:per_group].astype(jnp.bfloat16))
        gate_table_out = jnp.zeros((per_group + 1, TOP), jnp.bfloat16).at[flat_tokens, flat_choices].set(gate_grads.reshape(-1))
        gate_parts.append(gate_table_out[:per_group])
    token_grad = jnp.concatenate(grad_parts, axis=0)
    gate_grad = jnp.concatenate(gate_parts, axis=0)
    new_momentum_in = (0.9 * momentum_in.astype(jnp.float32) + sums_in).astype(jnp.bfloat16)
    new_momentum_out = (0.9 * momentum_out.astype(jnp.float32) + sums_out).astype(jnp.bfloat16)
    return token_grad, gate_grad, new_momentum_in, new_momentum_out
```

```python
import functools

import jax
import jax.numpy as jnp
from jax import lax
from jax.experimental import pallas as pl
from jax.experimental.pallas import tpu as pltpu
from jax.sharding import PartitionSpec as P


decay = 0.9
f32, bf16, i32 = jnp.float32, jnp.bfloat16, jnp.int32
PEERS, TOK, WIDTH, HALF, FFN, CAP, TOP, REPS = 128, 128, 1536, 768, 384, 5, 4, 4
ROWS = PEERS * CAP
UNIT = 16 * CAP
by_mesh = pl.DeviceIdType.MESH


def iota(shape, dim):
    return lax.broadcasted_iota(i32, shape, dim)


def dot(a, b, over=(1, 0)):
    return lax.dot_general(a, b, (((over[0],), (over[1],)), ((), ())), preferred_element_type=f32)


def kernel(
    tok_ref, routes_ref, gates_ref, dy_ref, w_in_ref, w_out_ref, mom_in_ref, mom_out_ref,
    token_grad_ref, gate_grad_ref, new_in_ref, new_out_ref,
    pick, pack, gate_rows, send, recv, back_send, back_recv,
    x_rows, scaled, dy_half, scale_col, win, wout, gate_up, hidden, dh, dgu, row_grad, gg,
    part_in, part_out, got_in, got_out,
    send_sem, recv_sem, back_send_sem, back_recv_sem, w_send, w_recv, in_send, in_recv, out_send, out_recv,
):
    rep = lax.axis_index("rep")
    me = lax.axis_index("expert")
    z, y, core = me // 16, (me // 2) % 8, me % 2

    def peer(j, sign):
        m = j // 2
        dz, dy, dc = m % 8, (m // 8 + m) % 8, j % 2
        return ((z + sign * dz + 8) % 8) * 16 + ((y + sign * dy + 8) % 8) * 2 + (core + dc) % 2

    barrier = pltpu.get_barrier_semaphore()

    @pl.loop(1, PEERS)
    def _(j):
        pl.semaphore_signal(barrier, inc=1, device_id=(rep, peer(j, 1)), device_id_type=by_mesh)

    for d in range(1, REPS):
        pl.semaphore_signal(barrier, inc=1, device_id=((rep + d) % REPS, me), device_id_type=by_mesh)

    expert_of = iota((PEERS, TOK), 0)
    before = (iota((TOK, TOK), 0) < iota((TOK, TOK), 1)).astype(f32).astype(bf16)
    base = jnp.zeros((PEERS, 1), f32)
    keys = []
    routes = routes_ref[...]
    gates = gates_ref[...].astype(f32)
    for k in range(TOP):
        route = routes[k : k + 1, :]
        named = (expert_of == route).astype(f32)
        count = dot(named.astype(bf16), before) + base
        slot = jnp.sum(named * count, axis=0, keepdims=True)
        base = base + jnp.sum(named, axis=1, keepdims=True)
        keys.append(route * 8 + slot.astype(i32))

    def key_of(j):
        m = j >> 1
        ez = (z + (m & 7)) & 7
        ey = (y + (((m >> 3) + m) & 7)) & 7
        return (ez * 16 + ey * 2 + ((core + (j & 1)) & 1)) * 8

    @pl.loop(0, 8)
    def _(q):
        r = iota((256, TOK), 0) & 15
        i = (r * 13) >> 6
        key = key_of(q * 16 + (iota((256, TOK), 0) >> 4)) + (r - i * 5)
        hit = functools.reduce(jnp.logical_or, [key == k for k in keys])
        for n in range(3):
            here = jnp.logical_and(hit, i == n)
            pick[pl.ds(q * 256, 256), n * 128 : (n + 1) * 128] = jnp.where(here, 1.0, 0.0).astype(bf16)

    own_key = key_of(iota((PEERS, TOK), 0))
    lane = iota((PEERS, 128), 1)
    rows = jnp.zeros((PEERS, 128), f32)
    for s in range(CAP):
        val = sum(jnp.where(own_key + s == keys[k], gates[k : k + 1, :], 0.0) for k in range(TOP))
        rows = rows + jnp.where(lane == s, jnp.sum(val, axis=1, keepdims=True), 0.0)
    gate_rows[...] = rows

    a, col = iota((4 * UNIT, 256), 0), iota((4 * UNIT, 256), 1)
    kind = (a >= UNIT).astype(i32) + (a >= 2 * UNIT).astype(i32) + (a >= 3 * UNIT).astype(i32)
    rr = a - kind * UNIT
    c16 = (rr * 205) >> 10
    want = c16 * 16 + jnp.where(kind == 3, 15, kind * 5 + rr - c16 * 5)
    pack[...] = (col == want).astype(f32).astype(bf16)

    u_iota = iota((UNIT, 128), 0)
    slot_lane = iota((UNIT, 128), 1) == u_iota - ((u_iota * 205) >> 10) * 5

    def gather(p):
        src, h = (tok_ref, p) if p < 2 else (dy_ref, p - 2)
        first = h * HALF
        blocks = [src[:, first + b * 128 : first + (b + 1) * 128] for b in range(6)]
        table = jnp.concatenate(
            [jnp.concatenate(blocks[0:3], axis=0), jnp.concatenate(blocks[3:6], axis=0)], axis=1
        )

        @pl.loop(0, 8)
        def _(q):
            out = dot(pick[pl.ds(q * 256, 256), :], table)
            left = out[:, :128].reshape(16, 16, 128)
            if p == 0:
                own = gate_rows[pl.ds(q * 16, 16), :].reshape(16, 1, 128)
                left = left + jnp.where(iota((16, 16, 128), 1) == 15, own, 0.0)
            send[p, pl.ds(q * 16, 16), 0:16, :] = left.astype(bf16)
            send[p, pl.ds(q * 16, 16), 16:32, :] = out[:, 128:].reshape(16, 16, 128).astype(bf16)

    def send_pass(p):
        pltpu.make_async_copy(send.at[p, 0], recv.at[p, 0], recv_sem.at[p]).start()

        @pl.loop(1, PEERS)
        def _(j):
            pltpu.make_async_remote_copy(
                send.at[p, j], recv.at[p, j], send_sem.at[p], recv_sem.at[p],
                device_id=(rep, peer(j, 1)), device_id_type=by_mesh,
            ).start()

    def send_back(h):
        pltpu.make_async_copy(back_send.at[h, 0], back_recv.at[h, 0], back_recv_sem.at[h]).start()

        @pl.loop(1, PEERS)
        def _(j):
            pltpu.make_async_remote_copy(
                back_send.at[h, j], back_recv.at[h, j], back_send_sem.at[h], back_recv_sem.at[h],
                device_id=(rep, peer(j, -1)), device_id_type=by_mesh,
            ).start()

    def wait_all(ref, sem):
        pltpu.make_async_copy(ref, ref, sem).wait()

    gather(0)
    pl.semaphore_wait(barrier, PEERS - 1 + REPS - 1)
    send_pass(0)

    mine = pl.ds(pl.multiple_of(rep * FFN, FFN), FFN)
    own_in = pltpu.make_async_copy(w_in_ref, win.at[mine], w_recv.at[0])
    own_out = pltpu.make_async_copy(w_out_ref, wout.at[rep], w_recv.at[1])
    own_in.start()
    own_out.start()
    for d in range(1, REPS):
        pltpu.make_async_remote_copy(
            w_in_ref, win.at[mine], w_send.at[0], w_recv.at[0],
            device_id=((rep + d) % REPS, me), device_id_type=by_mesh,
        ).start()
    for d in range(1, REPS):
        pltpu.make_async_remote_copy(
            w_out_ref, wout.at[rep], w_send.at[1], w_recv.at[1],
            device_id=((rep + d) % REPS, me), device_id_type=by_mesh,
        ).start()
    for p in range(1, 4):
        gather(p)
        send_pass(p)

    def unpack(p):
        wait_all(recv.at[p], recv_sem.at[p])
        first = (p % 2) * HALF

        @pl.loop(0, 8)
        def _(u):
            left = recv[p, pl.ds(u * 16, 16), 0:16, :].reshape(256, 128)
            right = recv[p, pl.ds(u * 16, 16), 16:32, :].reshape(256, 128)
            both = jnp.concatenate([left, right], axis=1)
            out = dot(pack[0 : 3 * UNIT, :], both)
            at = pl.ds(pl.multiple_of(u * UNIT, UNIT), UNIT)
            if p == 0:
                gate = jnp.where(slot_lane, dot(pack[3 * UNIT :, :], left), 0.0)
                scale_col[at, :] = jnp.broadcast_to(jnp.sum(gate, axis=1, keepdims=True), (UNIT, 128))
            for side in range(2):
                for i in range(3):
                    block = out[i * UNIT : (i + 1) * UNIT, side * 128 : (side + 1) * 128]
                    b = side * 3 + i
                    if p < 2:
                        x_rows[at, first + b * 128 : first + (b + 1) * 128] = block.astype(bf16)
                    else:
                        dy_half[at, b * 128 : (b + 1) * 128] = block.astype(bf16)
                        scaled[at, first + b * 128 : first + (b + 1) * 128] = (
                            scale_col[at, :] * block
                        ).astype(bf16)

    unpack(0)
    wait_all(win, w_recv.at[0])

    def project(h):
        @pl.loop(0, 3)
        def _(n):
            at = pl.ds(pl.multiple_of(n * 256, 256), 256)
            out = dot(x_rows[:, h * HALF : (h + 1) * HALF], win[h * HALF : (h + 1) * HALF, at])
            gate_up[:, at] = out if h == 0 else gate_up[:, at] + out

    project(0)
    unpack(1)
    project(1)

    @pl.loop(0, 8)
    def _(u):
        at = pl.ds(pl.multiple_of(u * UNIT, UNIT), UNIT)
        g, up = gate_up[at, :FFN], gate_up[at, FFN:]
        sigma = 1.0 / (1.0 + jnp.exp(-g))
        silu = g * sigma
        hidden[at, :] = (silu * up).astype(bf16)
        gate_up[at, :FFN] = up * sigma * (1.0 + g * (1.0 - sigma))
        gate_up[at, FFN:] = silu

    wait_all(wout, w_recv.at[1])

    def gate_sums(h):
        @pl.loop(0, 4)
        def _(q):
            at = pl.ds(pl.multiple_of(q * 160, 160), 160)
            total = jnp.zeros((160, 128), f32)
            for r in range(2):
                out = dot(hidden[at, :], wout[2 * h + r])
                for b in range(3):
                    c = r * 3 + b
                    total = total + out[:, b * 128 : (b + 1) * 128] * dy_half[
                        at, c * 128 : (c + 1) * 128
                    ].astype(f32)
            gg[at, :] = total if h == 0 else gg[at, :] + total

    def out_part(r):
        part_out[r] = dot(hidden[...], scaled[:, r * FFN : (r + 1) * FFN], (0, 0)).astype(bf16)

        @pl.when(rep != r)
        def _():
            slot = (rep - r + REPS - 1) % REPS
            pltpu.make_async_remote_copy(
                part_out.at[r], got_out.at[slot], out_send, out_recv.at[slot],
                device_id=(r, me), device_id_type=by_mesh,
            ).start()

    unpack(2)
    dh[...] = dot(scaled[:, 0:FFN], wout[0], (1, 1)) + dot(scaled[:, FFN:HALF], wout[1], (1, 1))
    out_part(0)
    out_part(1)
    gate_sums(0)

    unpack(3)
    for q in range(4):
        at = pl.ds(q * 160, 160)
        d = (
            dh[at, :]
            + dot(scaled[at, HALF : HALF + FFN], wout[2], (1, 1))
            + dot(scaled[at, HALF + FFN :], wout[3], (1, 1))
        )
        dgu[at, :FFN] = (d * gate_up[at, :FFN]).astype(bf16)
        dgu[at, FFN:] = (d * gate_up[at, FFN:]).astype(bf16)

    def back(h):
        @pl.loop(0, 3)
        def _(n):
            at = pl.ds(pl.multiple_of(n * 256, 256), 256)
            from_in = pl.ds(pl.multiple_of(h * HALF + n * 256, 256), 256)
            row_grad[:, at] = dot(dgu[...], win[from_in, :], (1, 1)).astype(bf16)

        @pl.loop(0, 8)
        def _(u):
            at = pl.ds(pl.multiple_of(u * UNIT, UNIT), UNIT)
            sides = []
            for side in range(2):
                parts = [row_grad[at, (side * 3 + i) * 128 : (side * 3 + i + 1) * 128] for i in range(3)]
                if h == 1:
                    gates_back = jnp.sum(gg[at, :], axis=1, keepdims=True)
                    here = jnp.where(slot_lane, gates_back, 0.0) if side else jnp.zeros((UNIT, 128), f32)
                    parts.append(here.astype(bf16))
                sides.append(jnp.concatenate(parts, axis=0))
            both = jnp.concatenate(sides, axis=1)
            out = dot(pack[0 : both.shape[0], :], both, (0, 0))
            back_send[h, pl.ds(u * 16, 16), 0:16, :] = out[:, :128].reshape(16, 16, 128).astype(bf16)
            back_send[h, pl.ds(u * 16, 16), 16:32, :] = out[:, 128:].reshape(16, 16, 128).astype(bf16)

        send_back(h)

    back(0)

    @pl.loop(1, REPS + 1)
    def _(d):
        r = (rep + d) % REPS
        at = pl.ds(pl.multiple_of(r * FFN, FFN), FFN)
        part_in[r] = dot(x_rows[:, at], dgu[...], (0, 0)).astype(bf16)

        @pl.when(d < REPS)
        def _():
            slot = (REPS - 1 + rep - r + REPS) % REPS
            pltpu.make_async_remote_copy(
                part_in.at[r], got_in.at[slot], in_send, in_recv.at[slot],
                device_id=(r, me), device_id_type=by_mesh,
            ).start()

    out_part(2)
    out_part(3)
    gate_sums(1)
    back(1)

    def combine(h):
        wait_all(back_recv.at[h], back_recv_sem.at[h])
        for side in range(2):
            total = dot(
                pick[...], back_recv[h, :, side * 16 : (side + 1) * 16, :].reshape(PEERS * 16, 128), (0, 0)
            )
            for i in range(3):
                b = h * 6 + side * 3 + i
                token_grad_ref[:, b * 128 : (b + 1) * 128] = total[i * TOK : (i + 1) * TOK, :].astype(bf16)

    combine(0)

    for s in range(REPS - 1):
        wait_all(got_out.at[s], out_recv.at[s])
    new_out_ref[...] = (
        decay * mom_out_ref[...].astype(f32)
        + part_out[rep].astype(f32)
        + sum(got_out[s].astype(f32) for s in range(REPS - 1))
    ).astype(bf16)
    for s in range(REPS - 1):
        wait_all(got_in.at[s], in_recv.at[s])
    new_in_ref[...] = (
        decay * mom_in_ref[...].astype(f32)
        + part_in[rep].astype(f32)
        + sum(got_in[s].astype(f32) for s in range(REPS - 1))
    ).astype(bf16)

    combine(1)
    last = back_recv[1, :, 16:32, :].astype(f32)
    got_gates = jnp.sum(jnp.where(iota((PEERS, 16, 128), 1) == 15, last, 0.0), axis=1)
    sums = [jnp.zeros((1, TOK), f32) for _ in range(TOP)]
    for s in range(CAP):
        value = jnp.sum(jnp.where(lane == s, got_gates, 0.0), axis=1, keepdims=True)
        for k in range(TOP):
            hit = own_key + s == keys[k]
            sums[k] = sums[k] + jnp.sum(jnp.where(hit, value, 0.0), axis=0, keepdims=True)
    gate_grad_ref[...] = jnp.concatenate(sums, axis=0).astype(bf16)

    for p in range(4):
        wait_all(send.at[p, pl.ds(1, PEERS - 1)], send_sem.at[p])
    for h in range(2):
        wait_all(back_send.at[h, pl.ds(1, PEERS - 1)], back_send_sem.at[h])
    wait_all(win.at[pl.ds(0, (REPS - 1) * FFN)], w_send.at[0])
    wait_all(wout.at[pl.ds(0, REPS - 1)], w_send.at[1])
    wait_all(part_in.at[pl.ds(0, REPS - 1)], in_send)
    wait_all(part_out.at[pl.ds(0, REPS - 1)], out_send)


def per_device(tokens, routes, gates, output_grad, w_in, w_out, momentum_in, momentum_out):
    vmem = pl.BlockSpec(memory_space=pltpu.VMEM)
    dma = pltpu.SemaphoreType.DMA
    scratch = [
        pltpu.VMEM((PEERS * 16, 3 * TOK), bf16),
        pltpu.VMEM((4 * UNIT, 256), bf16),
        pltpu.VMEM((PEERS, 128), f32),
        pltpu.VMEM((4, PEERS, 32, 128), bf16),
        pltpu.VMEM((4, PEERS, 32, 128), bf16),
        pltpu.VMEM((2, PEERS, 32, 128), bf16),
        pltpu.VMEM((2, PEERS, 32, 128), bf16),
        pltpu.VMEM((ROWS, WIDTH), bf16),
        pltpu.VMEM((ROWS, WIDTH), bf16),
        pltpu.VMEM((ROWS, HALF), bf16),
        pltpu.VMEM((ROWS, 128), f32),
        pltpu.VMEM((WIDTH, 2 * FFN), bf16),
        pltpu.VMEM((REPS, FFN, FFN), bf16),
        pltpu.VMEM((ROWS, 2 * FFN), f32),
        pltpu.VMEM((ROWS, FFN), bf16),
        pltpu.VMEM((ROWS, FFN), f32),
        pltpu.VMEM((ROWS, 2 * FFN), bf16),
        pltpu.VMEM((ROWS, HALF), bf16),
        pltpu.VMEM((ROWS, 128), f32),
        pltpu.VMEM((REPS, FFN, 2 * FFN), bf16),
        pltpu.VMEM((REPS, FFN, FFN), bf16),
        pltpu.VMEM((REPS - 1, FFN, 2 * FFN), bf16),
        pltpu.VMEM((REPS - 1, FFN, FFN), bf16),
        dma((4,)), dma((4,)), dma((2,)), dma((2,)), dma((2,)), dma((2,)),
        dma, dma((REPS - 1,)), dma, dma((REPS - 1,)),
    ]
    token_grad, gate_grad, new_in, new_out = pl.pallas_call(
        kernel,
        out_shape=(
            jax.ShapeDtypeStruct((TOK, WIDTH), bf16),
            jax.ShapeDtypeStruct((TOP, TOK), bf16),
            jax.ShapeDtypeStruct((FFN, 2 * FFN), bf16),
            jax.ShapeDtypeStruct((FFN, FFN), bf16),
        ),
        in_specs=[vmem] * 8,
        out_specs=(vmem,) * 4,
        scratch_shapes=scratch,
        compiler_params=pltpu.CompilerParams(
            collective_id=0, has_side_effects=True, vmem_limit_bytes=56 * 2**20
        ),
    )(tokens, routes.T, gates.T, output_grad, w_in[0], w_out[0], momentum_in[0], momentum_out[0])
    return token_grad, gate_grad.T, new_in[None], new_out[None]


def solution(mesh):
    rows, w_in, w_out = P(("rep", "expert"), None), P("expert", "rep", None), P("expert", None, "rep")
    return jax.shard_map(
        per_device,
        mesh=mesh,
        in_specs=(rows, rows, rows, rows, w_in, w_out, w_in, w_out),
        out_specs=(rows, rows, w_in, w_out),
        check_vma=False,
    )
```

```python
import functools

import jax
import jax.numpy as jnp
from jax import lax
from jax.experimental import pallas as pl
from jax.experimental.pallas import tpu as pltpu
from jax.sharding import PartitionSpec as P


decay = 0.9
f32, bf16, i32 = jnp.float32, jnp.bfloat16, jnp.int32
PEERS, TOK, WIDTH, HALF, FFN, CAP, TOP, REPS = 128, 128, 1536, 768, 384, 5, 4, 4
ROWS = PEERS * CAP
UNIT = 16 * CAP
GROUPS, MEMBERS = 2, 64
GROUP = MEMBERS * CAP
by_mesh = pl.DeviceIdType.MESH


def iota(shape, dim):
    return lax.broadcasted_iota(i32, shape, dim)


def dot(a, b, over=(1, 0)):
    return lax.dot_general(a, b, (((over[0],), (over[1],)), ((), ())), preferred_element_type=f32)


def kernel(
    tok_any, routes_ref, gates_ref, dy_any, w_in_ref, w_out_ref, mom_in_any, mom_out_any,
    token_grad_ref, gate_grad_ref, new_in_ref, new_out_ref,
    tok_ref, dy_ref, mom_in_ref, mom_out_ref, pick, pick_t, pack, gate_rows, send, recv, back_send, back_recv,
    x_rows, x_t, scaled, dy_half, scale_col, win, wout, gate_up, win_t, wout_t, hidden, dh, dgu, row_grad, gg,
    part_in, part_out, got_in, got_out,
    send_sem, recv_sem, back_send_sem, back_recv_sem, w_send, w_recv, in_send, in_recv, out_send, out_recv, layers_in, local,
):
    rep = lax.axis_index("rep")
    me = lax.axis_index("expert")
    z, y, core = me // 16, (me // 2) % 8, me % 2

    def peer(j, sign):
        m = j // 2
        dz, dy, dc = m % 8, (m // 8 + m) % 8, j % 2
        return ((z + sign * dz + 8) % 8) * 16 + ((y + sign * dy + 8) % 8) * 2 + (core + dc) % 2

    barrier = pltpu.get_barrier_semaphore()
    in_layer = me % 16

    def greet(sem, to_rep, to):
        pl.semaphore_signal(sem, inc=1, device_id=(to_rep, to), device_id_type=by_mesh)

    for d in range(1, 8):
        greet(barrier, rep, ((z + d) % 8) * 16 + in_layer)

    @pl.loop(1, 16)
    def _(d):
        greet(barrier, rep, z * 16 + (in_layer + d) % 16)

    for d in range(1, REPS):
        greet(barrier, (rep + d) % REPS, me)

    inputs = [
        pltpu.make_async_copy(a, b, local.at[n])
        for n, (a, b) in enumerate(
            [(tok_any, tok_ref), (dy_any, dy_ref), (mom_in_any, mom_in_ref), (mom_out_any, mom_out_ref)]
        )
    ]
    for copy in inputs:
        copy.start()

    expert_of = iota((PEERS, TOK), 0)
    before = (iota((TOK, TOK), 0) < iota((TOK, TOK), 1)).astype(f32).astype(bf16)
    base = jnp.zeros((PEERS, 1), f32)
    keys = []
    routes = routes_ref[...]
    gates = gates_ref[...].astype(f32)
    for k in range(TOP):
        route = routes[k : k + 1, :]
        named = (expert_of == route).astype(f32)
        count = dot(named.astype(bf16), before) + base
        slot = jnp.sum(named * count, axis=0, keepdims=True)
        base = base + jnp.sum(named, axis=1, keepdims=True)
        keys.append(route * 8 + slot.astype(i32))

    def key_of(j):
        m = j >> 1
        ez = (z + (m & 7)) & 7
        ey = (y + (((m >> 3) + m) & 7)) & 7
        return (ez * 16 + ey * 2 + ((core + (j & 1)) & 1)) * 8

    @pl.loop(0, 8)
    def _(q):
        r = iota((256, TOK), 0) & 15
        i = (r * 13) >> 6
        key = key_of(q * 16 + (iota((256, TOK), 0) >> 4)) + (r - i * 5)
        hit = functools.reduce(jnp.logical_or, [key == k for k in keys])
        for n in range(3):
            here = jnp.logical_and(hit, i == n)
            pick[pl.ds(q * 256, 256), n * 128 : (n + 1) * 128] = jnp.where(here, 1.0, 0.0).astype(bf16)

    own_key = key_of(iota((PEERS, TOK), 0))
    lane = iota((PEERS, 128), 1)
    rows = jnp.zeros((PEERS, 128), f32)
    for s in range(CAP):
        val = sum(jnp.where(own_key + s == keys[k], gates[k : k + 1, :], 0.0) for k in range(TOP))
        rows = rows + jnp.where(lane == s, jnp.sum(val, axis=1, keepdims=True), 0.0)
    gate_rows[...] = rows

    a, col = iota((4 * UNIT, 256), 0), iota((4 * UNIT, 256), 1)
    kind = (a >= UNIT).astype(i32) + (a >= 2 * UNIT).astype(i32) + (a >= 3 * UNIT).astype(i32)
    rr = a - kind * UNIT
    c16 = (rr * 205) >> 10
    want = c16 * 16 + jnp.where(kind == 3, 15, kind * 5 + rr - c16 * 5)
    pack[...] = (col == want).astype(f32).astype(bf16)

    u_iota = iota((UNIT, 128), 0)
    slot_lane = iota((UNIT, 128), 1) == u_iota - ((u_iota * 205) >> 10) * 5

    def gather(p):
        src, h = (tok_ref, p) if p < 2 else (dy_ref, p - 2)
        first = h * HALF
        blocks = [src[:, first + b * 128 : first + (b + 1) * 128] for b in range(6)]
        table = jnp.concatenate(
            [jnp.concatenate(blocks[0:3], axis=0), jnp.concatenate(blocks[3:6], axis=0)], axis=1
        )

        @pl.loop(0, 8)
        def _(q):
            out = dot(pick[pl.ds(q * 256, 256), :], table)
            left = out[:, :128].reshape(16, 16, 128)
            if p == 0:
                own = gate_rows[pl.ds(q * 16, 16), :].reshape(16, 1, 128)
                left = left + jnp.where(iota((16, 16, 128), 1) == 15, own, 0.0)
            send[p, pl.ds(q * 16, 16), 0:16, :] = left.astype(bf16)
            send[p, pl.ds(q * 16, 16), 16:32, :] = out[:, 128:].reshape(16, 16, 128).astype(bf16)

    def send_pass(p):
        for g in range(GROUPS):
            arrived = recv_sem.at[3 + g if p == 3 else p]
            if g == 0:
                pltpu.make_async_copy(send.at[p, 0], recv.at[p, 0], arrived).start()

            @pl.loop(max(1, g * MEMBERS), (g + 1) * MEMBERS)
            def _(j):
                pltpu.make_async_remote_copy(
                    send.at[p, j], recv.at[p, j], send_sem.at[p], arrived,
                    device_id=(rep, peer(j, 1)), device_id_type=by_mesh,
                ).start()

    def send_back(h, g):
        def one(j):
            pltpu.make_async_remote_copy(
                back_send.at[h, j], back_recv.at[h, j], back_send_sem.at[h], back_recv_sem.at[h],
                device_id=(rep, peer(j, -1)), device_id_type=by_mesh,
            ).start()

        @pl.when(g > 0)
        def _():
            one(g * MEMBERS)

        @pl.when(g == 0)
        def _():
            pltpu.make_async_copy(back_send.at[h, 0], back_recv.at[h, 0], back_recv_sem.at[h]).start()

        @pl.loop(1, MEMBERS)
        def _(i):
            one(g * MEMBERS + i)

    def wait_all(ref, sem):
        pltpu.make_async_copy(ref, ref, sem).wait()

    pl.semaphore_wait(barrier, 7 + 15 + REPS - 1)
    for d in range(1, 8):
        greet(layers_in, rep, ((z + d) % 8) * 16 + in_layer)
    inputs[0].wait()
    gather(0)
    pl.semaphore_wait(layers_in, 7)
    send_pass(0)

    mine = pl.ds(pl.multiple_of(rep * FFN, FFN), FFN)
    own_in = pltpu.make_async_copy(w_in_ref, win.at[mine], w_recv.at[0])
    own_out = pltpu.make_async_copy(w_out_ref, wout.at[rep], w_recv.at[1])
    own_in.start()
    own_out.start()
    for d in range(1, REPS):
        pltpu.make_async_remote_copy(
            w_in_ref, win.at[mine], w_send.at[0], w_recv.at[0],
            device_id=((rep + d) % REPS, me), device_id_type=by_mesh,
        ).start()
    for d in range(1, REPS):
        pltpu.make_async_remote_copy(
            w_out_ref, wout.at[rep], w_send.at[1], w_recv.at[1],
            device_id=((rep + d) % REPS, me), device_id_type=by_mesh,
        ).start()
    inputs[1].wait()
    for p in range(1, 4):
        gather(p)
        send_pass(p)

    def unpack(p, start=0, units=8):
        first = (p % 2) * HALF

        @pl.loop(0, units)
        def _(step):
            u = start + step
            left = recv[p, pl.ds(u * 16, 16), 0:16, :].reshape(256, 128)
            right = recv[p, pl.ds(u * 16, 16), 16:32, :].reshape(256, 128)
            both = jnp.concatenate([left, right], axis=1)
            out = dot(pack[0 : 3 * UNIT, :], both)
            at = pl.ds(pl.multiple_of(u * UNIT, UNIT), UNIT)
            if p == 0:
                gate = jnp.where(slot_lane, dot(pack[3 * UNIT :, :], left), 0.0)
                scale_col[at, :] = jnp.broadcast_to(jnp.sum(gate, axis=1, keepdims=True), (UNIT, 128))
            for side in range(2):
                for i in range(3):
                    block = out[i * UNIT : (i + 1) * UNIT, side * 128 : (side + 1) * 128]
                    b = side * 3 + i
                    if p < 2:
                        x_rows[at, first + b * 128 : first + (b + 1) * 128] = block.astype(bf16)
                    else:
                        dy_half[at, b * 128 : (b + 1) * 128] = block.astype(bf16)
                        scaled[at, first + b * 128 : first + (b + 1) * 128] = (
                            scale_col[at, :] * block
                        ).astype(bf16)

    wait_all(recv.at[0], recv_sem.at[0])
    unpack(0)
    wait_all(win, w_recv.at[0])

    def project(h):
        @pl.loop(0, 3)
        def _(n):
            at = pl.ds(pl.multiple_of(n * 256, 256), 256)
            out = dot(x_rows[:, h * HALF : (h + 1) * HALF], win[h * HALF : (h + 1) * HALF, at])
            gate_up[:, at] = out if h == 0 else gate_up[:, at] + out

    project(0)
    wait_all(recv.at[1], recv_sem.at[1])
    unpack(1)
    project(1)

    @pl.loop(0, REPS)
    def _(r):
        at = pl.ds(pl.multiple_of(r * FFN, FFN), FFN)
        x_t[at, :] = x_rows[:, at].T
        win_t[:, at] = win[at, :].T
        block = pl.ds(pl.multiple_of(r * 512, 512), 512)
        pick_t[:, block] = pick[block, :].T

    @pl.loop(0, 8)
    def _(u):
        at = pl.ds(pl.multiple_of(u * UNIT, UNIT), UNIT)
        g, up = gate_up[at, :FFN], gate_up[at, FFN:]
        sigma = 1.0 / (1.0 + jnp.exp(-g))
        silu = g * sigma
        hidden[at, :] = (silu * up).astype(bf16)
        gate_up[at, :FFN] = up * sigma * (1.0 + g * (1.0 - sigma))
        gate_up[at, FFN:] = silu

    wait_all(wout, w_recv.at[1])

    @pl.loop(0, REPS)
    def _(r):
        wout_t[r] = wout[r].T

    def gate_sums(h, g):
        at = pl.ds(pl.multiple_of(g * GROUP, GROUP), GROUP)
        total = jnp.zeros((GROUP, 128), f32) if h == 0 else gg[at, :]
        for r in range(2):
            out = dot(hidden[at, :], wout[2 * h + r])
            for b in range(3):
                c = r * 3 + b
                total = total + out[:, b * 128 : (b + 1) * 128] * dy_half[
                    at, c * 128 : (c + 1) * 128
                ].astype(f32)
        gg[at, :] = total

    def out_part(r):
        part_out[r] = dot(hidden[...], scaled[:, r * FFN : (r + 1) * FFN], (0, 0)).astype(bf16)

        @pl.when(rep != r)
        def _():
            slot = (rep - r + REPS - 1) % REPS
            pltpu.make_async_remote_copy(
                part_out.at[r], got_out.at[slot], out_send, out_recv.at[slot],
                device_id=(r, me), device_id_type=by_mesh,
            ).start()

    wait_all(recv.at[2], recv_sem.at[2])
    unpack(2)
    dh[...] = dot(scaled[:, 0:FFN], wout_t[0]) + dot(scaled[:, FFN:HALF], wout_t[1])
    out_part(0)
    out_part(1)
    pl.loop(0, GROUPS)(lambda g: gate_sums(0, g))

    def row_grads(h, g):
        rows = pl.ds(pl.multiple_of(g * GROUP, GROUP), GROUP)
        row_grad[rows, :] = dot(dgu[rows, :], win_t[:, h * HALF : (h + 1) * HALF]).astype(bf16)

        @pl.loop(0, GROUP // UNIT)
        def _(step):
            u = g * (GROUP // UNIT) + step
            at = pl.ds(pl.multiple_of(u * UNIT, UNIT), UNIT)
            sides = []
            for side in range(2):
                parts = [row_grad[at, (side * 3 + i) * 128 : (side * 3 + i + 1) * 128] for i in range(3)]
                if h == 1:
                    gates_back = jnp.sum(gg[at, :], axis=1, keepdims=True)
                    here = jnp.where(slot_lane, gates_back, 0.0) if side else jnp.zeros((UNIT, 128), f32)
                    parts.append(here.astype(bf16))
                sides.append(jnp.concatenate(parts, axis=0))
            both = jnp.concatenate(sides, axis=1)
            out = dot(pack[0 : both.shape[0], :], both, (0, 0))
            back_send[h, pl.ds(u * 16, 16), 0:16, :] = out[:, :128].reshape(16, 16, 128).astype(bf16)
            back_send[h, pl.ds(u * 16, 16), 16:32, :] = out[:, 128:].reshape(16, 16, 128).astype(bf16)

    def arrival(g):
        wait_all(recv.at[3, pl.ds(g * MEMBERS, MEMBERS)], recv_sem.at[3 + g])

    def first_half(g):
        unpack(3, g * (GROUP // UNIT), GROUP // UNIT)
        at = pl.ds(pl.multiple_of(g * GROUP, GROUP), GROUP)
        d = (
            dh[at, :]
            + dot(scaled[at, HALF : HALF + FFN], wout_t[2])
            + dot(scaled[at, HALF + FFN :], wout_t[3])
        )
        dgu[at, :FFN] = (d * gate_up[at, :FFN]).astype(bf16)
        dgu[at, FFN:] = (d * gate_up[at, FFN:]).astype(bf16)
        row_grads(0, g)

    def second_half(g):
        gate_sums(1, g)
        row_grads(1, g)

    @pl.loop(0, GROUPS)
    def _(g):
        arrival(g)

        @pl.when(g == GROUPS - 1)
        def _():
            pl.loop(0, GROUPS - 1)(lambda k: send_back(0, k))

        first_half(g)

        @pl.when(g < GROUPS - 1)
        def _():
            second_half(g)

    send_back(0, GROUPS - 1)

    @pl.loop(1, REPS)
    def _(d):
        r = (rep + d) % REPS
        part_in[r] = dot(x_t[pl.ds(pl.multiple_of(r * FFN, FFN), FFN), :], dgu[...]).astype(bf16)
        slot = REPS - 1 - d
        pltpu.make_async_remote_copy(
            part_in.at[r], got_in.at[slot], in_send, in_recv.at[slot],
            device_id=(r, me), device_id_type=by_mesh,
        ).start()

    second_half(GROUPS - 1)
    pl.loop(0, GROUPS)(lambda g: send_back(1, g))
    out_part(2)
    out_part(3)
    part_in[rep] = dot(x_t[mine, :], dgu[...]).astype(bf16)

    def combine(h):
        wait_all(back_recv.at[h], back_recv_sem.at[h])
        for side in range(2):
            total = dot(
                pick_t[...], back_recv[h, :, side * 16 : (side + 1) * 16, :].reshape(PEERS * 16, 128)
            )
            for i in range(3):
                b = h * 6 + side * 3 + i
                token_grad_ref[:, b * 128 : (b + 1) * 128] = total[i * TOK : (i + 1) * TOK, :].astype(bf16)

    combine(0)
    inputs[2].wait()
    inputs[3].wait()

    for s in range(REPS - 1):
        wait_all(got_out.at[s], out_recv.at[s])
    new_out_ref[...] = (
        decay * mom_out_ref[...].astype(f32)
        + part_out[rep].astype(f32)
        + sum(got_out[s].astype(f32) for s in range(REPS - 1))
    ).astype(bf16)
    for s in range(REPS - 1):
        wait_all(got_in.at[s], in_recv.at[s])
    new_in_ref[...] = (
        decay * mom_in_ref[...].astype(f32)
        + part_in[rep].astype(f32)
        + sum(got_in[s].astype(f32) for s in range(REPS - 1))
    ).astype(bf16)

    combine(1)
    last = back_recv[1, :, 16:32, :].astype(f32)
    got_gates = jnp.sum(jnp.where(iota((PEERS, 16, 128), 1) == 15, last, 0.0), axis=1)
    sums = [jnp.zeros((1, TOK), f32) for _ in range(TOP)]
    for s in range(CAP):
        value = jnp.sum(jnp.where(lane == s, got_gates, 0.0), axis=1, keepdims=True)
        for k in range(TOP):
            hit = own_key + s == keys[k]
            sums[k] = sums[k] + jnp.sum(jnp.where(hit, value, 0.0), axis=0, keepdims=True)
    gate_grad_ref[...] = jnp.concatenate(sums, axis=0).astype(bf16)

    for p in range(4):
        wait_all(send.at[p, pl.ds(1, PEERS - 1)], send_sem.at[p])
    for h in range(2):
        wait_all(back_send.at[h, pl.ds(1, PEERS - 1)], back_send_sem.at[h])
    wait_all(win.at[pl.ds(0, (REPS - 1) * FFN)], w_send.at[0])
    wait_all(wout.at[pl.ds(0, REPS - 1)], w_send.at[1])
    wait_all(part_in.at[pl.ds(0, REPS - 1)], in_send)
    wait_all(part_out.at[pl.ds(0, REPS - 1)], out_send)


def per_device(tokens, routes, gates, output_grad, w_in, w_out, momentum_in, momentum_out):
    vmem = pl.BlockSpec(memory_space=pltpu.VMEM)
    dma = pltpu.SemaphoreType.DMA
    any_space = pl.BlockSpec(memory_space=pl.ANY)
    scratch = [
        pltpu.VMEM((TOK, WIDTH), bf16),
        pltpu.VMEM((TOK, WIDTH), bf16),
        pltpu.VMEM((FFN, 2 * FFN), bf16),
        pltpu.VMEM((FFN, FFN), bf16),
        pltpu.VMEM((PEERS * 16, 3 * TOK), bf16),
        pltpu.VMEM((3 * TOK, PEERS * 16), bf16),
        pltpu.VMEM((4 * UNIT, 256), bf16),
        pltpu.VMEM((PEERS, 128), f32),
        pltpu.VMEM((4, PEERS, 32, 128), bf16),
        pltpu.VMEM((4, PEERS, 32, 128), bf16),
        pltpu.VMEM((2, PEERS, 32, 128), bf16),
        pltpu.VMEM((2, PEERS, 32, 128), bf16),
        pltpu.VMEM((ROWS, WIDTH), bf16),
        pltpu.VMEM((WIDTH, ROWS), bf16),
        pltpu.VMEM((ROWS, WIDTH), bf16),
        pltpu.VMEM((ROWS, HALF), bf16),
        pltpu.VMEM((ROWS, 128), f32),
        pltpu.VMEM((WIDTH, 2 * FFN), bf16),
        pltpu.VMEM((REPS, FFN, FFN), bf16),
        pltpu.VMEM((ROWS, 2 * FFN), f32),
        pltpu.VMEM((2 * FFN, WIDTH), bf16),
        pltpu.VMEM((REPS, FFN, FFN), bf16),
        pltpu.VMEM((ROWS, FFN), bf16),
        pltpu.VMEM((ROWS, FFN), f32),
        pltpu.VMEM((ROWS, 2 * FFN), bf16),
        pltpu.VMEM((ROWS, HALF), bf16),
        pltpu.VMEM((ROWS, 128), f32),
        pltpu.VMEM((REPS, FFN, 2 * FFN), bf16),
        pltpu.VMEM((REPS, FFN, FFN), bf16),
        pltpu.VMEM((REPS - 1, FFN, 2 * FFN), bf16),
        pltpu.VMEM((REPS - 1, FFN, FFN), bf16),
        dma((4,)), dma((3 + GROUPS,)), dma((2,)), dma((2,)), dma((2,)), dma((2,)),
        dma, dma((REPS - 1,)), dma, dma((REPS - 1,)), pltpu.SemaphoreType.REGULAR, dma((4,)),
    ]
    token_grad, gate_grad, new_in, new_out = pl.pallas_call(
        kernel,
        out_shape=(
            pltpu.VMEM((TOK, WIDTH), bf16),
            pltpu.VMEM((TOP, TOK), bf16),
            pltpu.VMEM((FFN, 2 * FFN), bf16),
            pltpu.VMEM((FFN, FFN), bf16),
        ),
        in_specs=[any_space, vmem, vmem] + [any_space] * 5,
        out_specs=(vmem,) * 4,
        scratch_shapes=scratch,
        compiler_params=pltpu.CompilerParams(
            collective_id=0, has_side_effects=True, vmem_limit_bytes=56 * 2**20
        ),
    )(tokens, routes.T, gates.T, output_grad, w_in[0], w_out[0], momentum_in[0], momentum_out[0])
    return token_grad, gate_grad.T, new_in[None], new_out[None]


def solution(mesh):
    rows, w_in, w_out = P(("rep", "expert"), None), P("expert", "rep", None), P("expert", None, "rep")
    return jax.shard_map(
        per_device,
        mesh=mesh,
        in_specs=(rows, rows, rows, rows, w_in, w_out, w_in, w_out),
        out_specs=(rows, rows, w_in, w_out),
        check_vma=False,
    )
```

```python
import functools

import jax
import jax.numpy as jnp
from jax import lax
from jax.experimental import pallas as pl
from jax.experimental.pallas import tpu as pltpu
from jax.sharding import PartitionSpec as P


decay = 0.9
f32, bf16, i32 = jnp.float32, jnp.bfloat16, jnp.int32
PEERS, TOK, WIDTH, HALF, FFN, CAP, TOP, REPS = 128, 128, 1536, 768, 384, 5, 4, 4
ROWS = PEERS * CAP
UNIT = 16 * CAP
GROUPS, MEMBERS = 2, 64
GROUP = MEMBERS * CAP
by_mesh = pl.DeviceIdType.MESH


def iota(shape, dim):
    return lax.broadcasted_iota(i32, shape, dim)


def dot(a, b, over=(1, 0)):
    return lax.dot_general(a, b, (((over[0],), (over[1],)), ((), ())), preferred_element_type=f32)


def kernel(
    tok_any, routes_ref, gates_ref, dy_any, w_in_ref, w_out_ref, mom_in_any, mom_out_any,
    token_grad_ref, gate_grad_ref, new_in_ref, new_out_ref,
    tok_ref, dy_ref, mom_in_ref, mom_out_ref, pick, pick_t, pack, gate_rows, send, recv, back_send, back_recv,
    x_rows, x_t, scaled, dy_half, scale_col, win, wout, gate_up, win_t, wout_t, hidden, dh, dgu, row_grad, gg,
    part_in, part_out, got_in, got_out,
    send_sem, recv_sem, back_send_sem, back_recv_sem, w_send, w_recv, in_send, in_recv, out_send, out_recv, layers_in, local,
):
    rep = lax.axis_index("rep")
    me = lax.axis_index("expert")
    z, y, core = me // 16, (me // 2) % 8, me % 2

    def peer(j, sign):
        m = j // 2
        dz, dy, dc = (m % 2) * 4 + (m % 8) // 2, (m // 8 + m) % 8, j % 2
        return ((z + sign * dz + 8) % 8) * 16 + ((y + sign * dy + 8) % 8) * 2 + (core + dc) % 2

    barrier = pltpu.get_barrier_semaphore()
    in_layer = me % 16

    def greet(sem, to_rep, to):
        pl.semaphore_signal(sem, inc=1, device_id=(to_rep, to), device_id_type=by_mesh)

    for d in range(1, 8):
        greet(barrier, rep, ((z + d) % 8) * 16 + in_layer)

    @pl.loop(1, 16)
    def _(d):
        greet(barrier, rep, z * 16 + (in_layer + d) % 16)

    for d in range(1, REPS):
        greet(barrier, (rep + d) % REPS, me)

    inputs = [
        pltpu.make_async_copy(a, b, local.at[n])
        for n, (a, b) in enumerate(
            [(tok_any, tok_ref), (dy_any, dy_ref), (mom_in_any, mom_in_ref), (mom_out_any, mom_out_ref)]
        )
    ]
    for copy in inputs:
        copy.start()

    expert_of = iota((PEERS, TOK), 0)
    before = (iota((TOK, TOK), 0) < iota((TOK, TOK), 1)).astype(f32).astype(bf16)
    base = jnp.zeros((PEERS, 1), f32)
    keys = []
    routes = routes_ref[...]
    gates = gates_ref[...].astype(f32)
    for k in range(TOP):
        route = routes[k : k + 1, :]
        named = (expert_of == route).astype(f32)
        count = dot(named.astype(bf16), before) + base
        slot = jnp.sum(named * count, axis=0, keepdims=True)
        base = base + jnp.sum(named, axis=1, keepdims=True)
        keys.append(route * 8 + slot.astype(i32))

    def key_of(j):
        m = j >> 1
        ez = (z + ((m & 1) * 4 + ((m & 7) >> 1))) & 7
        ey = (y + (((m >> 3) + m) & 7)) & 7
        return (ez * 16 + ey * 2 + ((core + (j & 1)) & 1)) * 8

    @pl.loop(0, 8)
    def _(q):
        r = iota((256, TOK), 0) & 15
        i = (r * 13) >> 6
        key = key_of(q * 16 + (iota((256, TOK), 0) >> 4)) + (r - i * 5)
        hit = functools.reduce(jnp.logical_or, [key == k for k in keys])
        for n in range(3):
            here = jnp.logical_and(hit, i == n)
            pick[pl.ds(q * 256, 256), n * 128 : (n + 1) * 128] = jnp.where(here, 1.0, 0.0).astype(bf16)

    own_key = key_of(iota((PEERS, TOK), 0))
    lane = iota((PEERS, 128), 1)
    rows = jnp.zeros((PEERS, 128), f32)
    for s in range(CAP):
        val = sum(jnp.where(own_key + s == keys[k], gates[k : k + 1, :], 0.0) for k in range(TOP))
        rows = rows + jnp.where(lane == s, jnp.sum(val, axis=1, keepdims=True), 0.0)
    gate_rows[...] = rows

    a, col = iota((4 * UNIT, 256), 0), iota((4 * UNIT, 256), 1)
    kind = (a >= UNIT).astype(i32) + (a >= 2 * UNIT).astype(i32) + (a >= 3 * UNIT).astype(i32)
    rr = a - kind * UNIT
    c16 = (rr * 205) >> 10
    want = c16 * 16 + jnp.where(kind == 3, 15, kind * 5 + rr - c16 * 5)
    pack[...] = (col == want).astype(f32).astype(bf16)

    u_iota = iota((UNIT, 128), 0)
    slot_lane = iota((UNIT, 128), 1) == u_iota - ((u_iota * 205) >> 10) * 5

    def gather(p):
        src, h = (tok_ref, p) if p < 2 else (dy_ref, p - 2)
        first = h * HALF
        blocks = [src[:, first + b * 128 : first + (b + 1) * 128] for b in range(6)]
        table = jnp.concatenate(
            [jnp.concatenate(blocks[0:3], axis=0), jnp.concatenate(blocks[3:6], axis=0)], axis=1
        )

        @pl.loop(0, 8)
        def _(q):
            out = dot(pick[pl.ds(q * 256, 256), :], table)
            left = out[:, :128].reshape(16, 16, 128)
            if p == 0:
                own = gate_rows[pl.ds(q * 16, 16), :].reshape(16, 1, 128)
                left = left + jnp.where(iota((16, 16, 128), 1) == 15, own, 0.0)
            send[p, pl.ds(q * 16, 16), 0:16, :] = left.astype(bf16)
            send[p, pl.ds(q * 16, 16), 16:32, :] = out[:, 128:].reshape(16, 16, 128).astype(bf16)

    def send_pass(p):
        for g in range(GROUPS):
            arrived = recv_sem.at[3 + g if p == 3 else p]
            if g == 0:
                pltpu.make_async_copy(send.at[p, 0], recv.at[p, 0], arrived).start()

            @pl.loop(max(1, g * MEMBERS), (g + 1) * MEMBERS)
            def _(j):
                pltpu.make_async_remote_copy(
                    send.at[p, j], recv.at[p, j], send_sem.at[p], arrived,
                    device_id=(rep, peer(j, 1)), device_id_type=by_mesh,
                ).start()

    def send_back(h, g):
        def one(j):
            pltpu.make_async_remote_copy(
                back_send.at[h, j], back_recv.at[h, j], back_send_sem.at[h], back_recv_sem.at[h],
                device_id=(rep, peer(j, -1)), device_id_type=by_mesh,
            ).start()

        @pl.when(g > 0)
        def _():
            one(g * MEMBERS)

        @pl.when(g == 0)
        def _():
            pltpu.make_async_copy(back_send.at[h, 0], back_recv.at[h, 0], back_recv_sem.at[h]).start()

        @pl.loop(1, MEMBERS)
        def _(i):
            one(g * MEMBERS + i)

    def wait_all(ref, sem):
        pltpu.make_async_copy(ref, ref, sem).wait()

    pl.semaphore_wait(barrier, 7 + 15 + REPS - 1)
    for d in range(1, 8):
        greet(layers_in, rep, ((z + d) % 8) * 16 + in_layer)
    inputs[0].wait()
    gather(0)
    pl.semaphore_wait(layers_in, 7)
    send_pass(0)

    mine = pl.ds(pl.multiple_of(rep * FFN, FFN), FFN)
    own_in = pltpu.make_async_copy(w_in_ref, win.at[mine], w_recv.at[0])
    own_out = pltpu.make_async_copy(w_out_ref, wout.at[rep], w_recv.at[1])
    own_in.start()
    own_out.start()
    for d in range(1, REPS):
        pltpu.make_async_remote_copy(
            w_in_ref, win.at[mine], w_send.at[0], w_recv.at[0],
            device_id=((rep + d) % REPS, me), device_id_type=by_mesh,
        ).start()
    for d in range(1, REPS):
        pltpu.make_async_remote_copy(
            w_out_ref, wout.at[rep], w_send.at[1], w_recv.at[1],
            device_id=((rep + d) % REPS, me), device_id_type=by_mesh,
        ).start()
    inputs[1].wait()
    for p in range(1, 4):
        gather(p)
        send_pass(p)

    def unpack(p, start=0, units=8):
        first = (p % 2) * HALF

        @pl.loop(0, units)
        def _(step):
            u = start + step
            left = recv[p, pl.ds(u * 16, 16), 0:16, :].reshape(256, 128)
            right = recv[p, pl.ds(u * 16, 16), 16:32, :].reshape(256, 128)
            both = jnp.concatenate([left, right], axis=1)
            out = dot(pack[0 : 3 * UNIT, :], both)
            at = pl.ds(pl.multiple_of(u * UNIT, UNIT), UNIT)
            if p == 0:
                gate = jnp.where(slot_lane, dot(pack[3 * UNIT :, :], left), 0.0)
                scale_col[at, :] = jnp.broadcast_to(jnp.sum(gate, axis=1, keepdims=True), (UNIT, 128))
            for side in range(2):
                for i in range(3):
                    block = out[i * UNIT : (i + 1) * UNIT, side * 128 : (side + 1) * 128]
                    b = side * 3 + i
                    if p < 2:
                        x_rows[at, first + b * 128 : first + (b + 1) * 128] = block.astype(bf16)
                    else:
                        dy_half[at, b * 128 : (b + 1) * 128] = block.astype(bf16)
                        scaled[at, first + b * 128 : first + (b + 1) * 128] = (
                            scale_col[at, :] * block
                        ).astype(bf16)

    wait_all(recv.at[0], recv_sem.at[0])
    unpack(0)
    wait_all(win, w_recv.at[0])

    def project(h):
        @pl.loop(0, 3)
        def _(n):
            at = pl.ds(pl.multiple_of(n * 256, 256), 256)
            out = dot(x_rows[:, h * HALF : (h + 1) * HALF], win[h * HALF : (h + 1) * HALF, at])
            gate_up[:, at] = out if h == 0 else gate_up[:, at] + out

    project(0)
    wait_all(recv.at[1], recv_sem.at[1])
    unpack(1)
    project(1)

    @pl.loop(0, REPS)
    def _(r):
        at = pl.ds(pl.multiple_of(r * FFN, FFN), FFN)
        x_t[at, :] = x_rows[:, at].T
        win_t[:, at] = win[at, :].T
        block = pl.ds(pl.multiple_of(r * 512, 512), 512)
        pick_t[:, block] = pick[block, :].T

    @pl.loop(0, 8)
    def _(u):
        at = pl.ds(pl.multiple_of(u * UNIT, UNIT), UNIT)
        g, up = gate_up[at, :FFN], gate_up[at, FFN:]
        sigma = 1.0 / (1.0 + jnp.exp(-g))
        silu = g * sigma
        hidden[at, :] = (silu * up).astype(bf16)
        gate_up[at, :FFN] = up * sigma * (1.0 + g * (1.0 - sigma))
        gate_up[at, FFN:] = silu

    wait_all(wout, w_recv.at[1])

    @pl.loop(0, REPS)
    def _(r):
        wout_t[r] = wout[r].T

    def gate_sums(h, g):
        at = pl.ds(pl.multiple_of(g * GROUP, GROUP), GROUP)
        total = jnp.zeros((GROUP, 128), f32) if h == 0 else gg[at, :]
        for r in range(2):
            out = dot(hidden[at, :], wout[2 * h + r])
            for b in range(3):
                c = r * 3 + b
                total = total + out[:, b * 128 : (b + 1) * 128] * dy_half[
                    at, c * 128 : (c + 1) * 128
                ].astype(f32)
        gg[at, :] = total

    def out_part(r):
        part_out[r] = dot(hidden[...], scaled[:, r * FFN : (r + 1) * FFN], (0, 0)).astype(bf16)

        @pl.when(rep != r)
        def _():
            slot = (rep - r + REPS - 1) % REPS
            pltpu.make_async_remote_copy(
                part_out.at[r], got_out.at[slot], out_send, out_recv.at[slot],
                device_id=(r, me), device_id_type=by_mesh,
            ).start()

    wait_all(recv.at[2], recv_sem.at[2])
    unpack(2)
    dh[...] = dot(scaled[:, 0:FFN], wout_t[0]) + dot(scaled[:, FFN:HALF], wout_t[1])
    out_part(0)
    out_part(1)
    pl.loop(0, GROUPS)(lambda g: gate_sums(0, g))

    def row_grads(h, g):
        rows = pl.ds(pl.multiple_of(g * GROUP, GROUP), GROUP)
        row_grad[rows, :] = dot(dgu[rows, :], win_t[:, h * HALF : (h + 1) * HALF]).astype(bf16)

        @pl.loop(0, GROUP // UNIT)
        def _(step):
            u = g * (GROUP // UNIT) + step
            at = pl.ds(pl.multiple_of(u * UNIT, UNIT), UNIT)
            sides = []
            for side in range(2):
                parts = [row_grad[at, (side * 3 + i) * 128 : (side * 3 + i + 1) * 128] for i in range(3)]
                if h == 1:
                    gates_back = jnp.sum(gg[at, :], axis=1, keepdims=True)
                    here = jnp.where(slot_lane, gates_back, 0.0) if side else jnp.zeros((UNIT, 128), f32)
                    parts.append(here.astype(bf16))
                sides.append(jnp.concatenate(parts, axis=0))
            both = jnp.concatenate(sides, axis=1)
            out = dot(pack[0 : both.shape[0], :], both, (0, 0))
            back_send[h, pl.ds(u * 16, 16), 0:16, :] = out[:, :128].reshape(16, 16, 128).astype(bf16)
            back_send[h, pl.ds(u * 16, 16), 16:32, :] = out[:, 128:].reshape(16, 16, 128).astype(bf16)

    def arrival(g):
        wait_all(recv.at[3, pl.ds(g * MEMBERS, MEMBERS)], recv_sem.at[3 + g])

    def first_half(g):
        unpack(3, g * (GROUP // UNIT), GROUP // UNIT)
        at = pl.ds(pl.multiple_of(g * GROUP, GROUP), GROUP)
        d = (
            dh[at, :]
            + dot(scaled[at, HALF : HALF + FFN], wout_t[2])
            + dot(scaled[at, HALF + FFN :], wout_t[3])
        )
        dgu[at, :FFN] = (d * gate_up[at, :FFN]).astype(bf16)
        dgu[at, FFN:] = (d * gate_up[at, FFN:]).astype(bf16)
        row_grads(0, g)

    def second_half(g):
        gate_sums(1, g)
        row_grads(1, g)

    @pl.loop(0, GROUPS)
    def _(g):
        arrival(g)

        @pl.when(g == GROUPS - 1)
        def _():
            pl.loop(0, GROUPS - 1)(lambda k: send_back(0, k))

        first_half(g)

        @pl.when(g < GROUPS - 1)
        def _():
            second_half(g)

    send_back(0, GROUPS - 1)

    @pl.loop(1, REPS)
    def _(d):
        r = (rep + d) % REPS
        part_in[r] = dot(x_t[pl.ds(pl.multiple_of(r * FFN, FFN), FFN), :], dgu[...]).astype(bf16)
        slot = REPS - 1 - d
        pltpu.make_async_remote_copy(
            part_in.at[r], got_in.at[slot], in_send, in_recv.at[slot],
            device_id=(r, me), device_id_type=by_mesh,
        ).start()

    second_half(GROUPS - 1)
    pl.loop(0, GROUPS)(lambda g: send_back(1, g))
    out_part(2)
    out_part(3)
    part_in[rep] = dot(x_t[mine, :], dgu[...]).astype(bf16)

    def combine(h):
        wait_all(back_recv.at[h], back_recv_sem.at[h])
        for side in range(2):
            total = dot(
                pick_t[...], back_recv[h, :, side * 16 : (side + 1) * 16, :].reshape(PEERS * 16, 128)
            )
            for i in range(3):
                b = h * 6 + side * 3 + i
                token_grad_ref[:, b * 128 : (b + 1) * 128] = total[i * TOK : (i + 1) * TOK, :].astype(bf16)

    combine(0)
    inputs[2].wait()
    inputs[3].wait()

    for s in range(REPS - 1):
        wait_all(got_out.at[s], out_recv.at[s])
    new_out_ref[...] = (
        decay * mom_out_ref[...].astype(f32)
        + part_out[rep].astype(f32)
        + sum(got_out[s].astype(f32) for s in range(REPS - 1))
    ).astype(bf16)
    for s in range(REPS - 1):
        wait_all(got_in.at[s], in_recv.at[s])
    new_in_ref[...] = (
        decay * mom_in_ref[...].astype(f32)
        + part_in[rep].astype(f32)
        + sum(got_in[s].astype(f32) for s in range(REPS - 1))
    ).astype(bf16)

    combine(1)
    last = back_recv[1, :, 16:32, :].astype(f32)
    got_gates = jnp.sum(jnp.where(iota((PEERS, 16, 128), 1) == 15, last, 0.0), axis=1)
    sums = [jnp.zeros((1, TOK), f32) for _ in range(TOP)]
    for s in range(CAP):
        value = jnp.sum(jnp.where(lane == s, got_gates, 0.0), axis=1, keepdims=True)
        for k in range(TOP):
            hit = own_key + s == keys[k]
            sums[k] = sums[k] + jnp.sum(jnp.where(hit, value, 0.0), axis=0, keepdims=True)
    gate_grad_ref[...] = jnp.concatenate(sums, axis=0).astype(bf16)

    for p in range(4):
        wait_all(send.at[p, pl.ds(1, PEERS - 1)], send_sem.at[p])
    for h in range(2):
        wait_all(back_send.at[h, pl.ds(1, PEERS - 1)], back_send_sem.at[h])
    wait_all(win.at[pl.ds(0, (REPS - 1) * FFN)], w_send.at[0])
    wait_all(wout.at[pl.ds(0, REPS - 1)], w_send.at[1])
    wait_all(part_in.at[pl.ds(0, REPS - 1)], in_send)
    wait_all(part_out.at[pl.ds(0, REPS - 1)], out_send)


def per_device(tokens, routes, gates, output_grad, w_in, w_out, momentum_in, momentum_out):
    vmem = pl.BlockSpec(memory_space=pltpu.VMEM)
    dma = pltpu.SemaphoreType.DMA
    any_space = pl.BlockSpec(memory_space=pl.ANY)
    scratch = [
        pltpu.VMEM((TOK, WIDTH), bf16),
        pltpu.VMEM((TOK, WIDTH), bf16),
        pltpu.VMEM((FFN, 2 * FFN), bf16),
        pltpu.VMEM((FFN, FFN), bf16),
        pltpu.VMEM((PEERS * 16, 3 * TOK), bf16),
        pltpu.VMEM((3 * TOK, PEERS * 16), bf16),
        pltpu.VMEM((4 * UNIT, 256), bf16),
        pltpu.VMEM((PEERS, 128), f32),
        pltpu.VMEM((4, PEERS, 32, 128), bf16),
        pltpu.VMEM((4, PEERS, 32, 128), bf16),
        pltpu.VMEM((2, PEERS, 32, 128), bf16),
        pltpu.VMEM((2, PEERS, 32, 128), bf16),
        pltpu.VMEM((ROWS, WIDTH), bf16),
        pltpu.VMEM((WIDTH, ROWS), bf16),
        pltpu.VMEM((ROWS, WIDTH), bf16),
        pltpu.VMEM((ROWS, HALF), bf16),
        pltpu.VMEM((ROWS, 128), f32),
        pltpu.VMEM((WIDTH, 2 * FFN), bf16),
        pltpu.VMEM((REPS, FFN, FFN), bf16),
        pltpu.VMEM((ROWS, 2 * FFN), f32),
        pltpu.VMEM((2 * FFN, WIDTH), bf16),
        pltpu.VMEM((REPS, FFN, FFN), bf16),
        pltpu.VMEM((ROWS, FFN), bf16),
        pltpu.VMEM((ROWS, FFN), f32),
        pltpu.VMEM((ROWS, 2 * FFN), bf16),
        pltpu.VMEM((ROWS, HALF), bf16),
        pltpu.VMEM((ROWS, 128), f32),
        pltpu.VMEM((REPS, FFN, 2 * FFN), bf16),
        pltpu.VMEM((REPS, FFN, FFN), bf16),
        pltpu.VMEM((REPS - 1, FFN, 2 * FFN), bf16),
        pltpu.VMEM((REPS - 1, FFN, FFN), bf16),
        dma((4,)), dma((3 + GROUPS,)), dma((2,)), dma((2,)), dma((2,)), dma((2,)),
        dma, dma((REPS - 1,)), dma, dma((REPS - 1,)), pltpu.SemaphoreType.REGULAR, dma((4,)),
    ]
    token_grad, gate_grad, new_in, new_out = pl.pallas_call(
        kernel,
        out_shape=(
            pltpu.VMEM((TOK, WIDTH), bf16),
            pltpu.VMEM((TOP, TOK), bf16),
            pltpu.VMEM((FFN, 2 * FFN), bf16),
            pltpu.VMEM((FFN, FFN), bf16),
        ),
        in_specs=[any_space, vmem, vmem] + [any_space] * 5,
        out_specs=(vmem,) * 4,
        scratch_shapes=scratch,
        compiler_params=pltpu.CompilerParams(
            collective_id=0, has_side_effects=True, vmem_limit_bytes=56 * 2**20
        ),
    )(tokens, routes.T, gates.T, output_grad, w_in[0], w_out[0], momentum_in[0], momentum_out[0])
    return token_grad, gate_grad.T, new_in[None], new_out[None]


def solution(mesh):
    rows, w_in, w_out = P(("rep", "expert"), None), P("expert", "rep", None), P("expert", None, "rep")
    return jax.shard_map(
        per_device,
        mesh=mesh,
        in_specs=(rows, rows, rows, rows, w_in, w_out, w_in, w_out),
        out_specs=(rows, rows, w_in, w_out),
        check_vma=False,
    )
```
